32 devices in a mesh: parts: 2 (over y), row: 4 (over z), col: 4 (over x, core).
Axes of the slice: x: 2, y: 2, z: 4, core: 2. Of those that a mesh axis runs over, the one named last changes fastest.
Arguments:
- pair: bfloat16 [384, 192, 128], P(('parts', 'row'), 'col'), parts along dimension 0, may hold values from -6 to 6
- mask: int32 [384], P('parts'), parts along dimension 0, may hold values 0 or 1
- in_weights: bfloat16 [128, 512], replicated, may hold values from -0.5 to 0.5
- gate_weight: bfloat16 [128, 128], replicated, may hold values from -0.5 to 0.5
- out_weight: bfloat16 [128, 128], replicated, may hold values from -0.5 to 0.5
Outputs:
- update: bfloat16 [384, 192, 128], P(('parts', 'row'), 'col'), parts along dimension 0
The draws below stay inside these ranges and needn't reach their ends.
There are 2 independent parts, one for each index of `parts`. The reference program is written for one: setup_inputs(seed, part) draws one part's arguments, and reference() takes and returns one part's arrays. A program takes and returns all parts, laid end to end along the dimension named above; an argument that names none is the same for every part. Nothing has to cross between parts.
Inputs may be any that keep to these rules, and one draw needn't show every extreme that they name: `mask`: 1 for a real residue, 0 for padding.
All inputs are finite; a program needn't handle non-finite values.
Results may differ from the reference program's by a relative error of at most 0.008.
Values may be sent and summed in bfloat16 or wider, within the bound.
A program may use at most 128 MiB of HBM per device.

```python
import jax
import jax.numpy as jnp
from jax import lax

C = 128
H = 128
N = 192


def set_ends(entries, own_key, least, largest):
    spot = [jax.random.randint(jax.random.fold_in(own_key, axis), (), 0, length) for axis, length in enumerate(entries.shape)]
    widest = entries.shape.index(max(entries.shape))
    neighbour = spot[:widest] + [(spot[widest] + 1) % entries.shape[widest]] + spot[widest + 1:]
    return entries.at[tuple(spot)].set(least).at[tuple(neighbour)].set(largest)


def block_levels(stream_key, shape, cuts, low, top_value):
    factor_of, own = 1.0, jax.random.fold_in(stream_key, 6)
    for dim, blocks in cuts:
        heights = jnp.exp(jax.random.uniform(jax.random.fold_in(own, dim), (blocks,), jnp.float32, low / len(cuts), top_value / len(cuts)))
        factor_of = factor_of * jnp.repeat(heights, shape[dim] // blocks).reshape([-1 if axis == dim else 1 for axis in range(len(shape))])
    return factor_of


def bell_draw(own_key, extent, width, reach, pieces=(), kind=jnp.bfloat16):
    drawn = width * jax.random.normal(own_key, extent, jnp.float32)
    if pieces:
        drawn = drawn * block_levels(own_key, extent, pieces, -0.22, 0.18)
    return jnp.clip(drawn, -reach, reach).astype(kind)


def setup_inputs(seed: int = 0, part: int = 0) -> dict:
    streams_of = jax.random.split(jax.random.key(seed), 6)
    part_splits = jax.random.split(jax.random.fold_in(streams_of[5], part), 6)
    pair = bell_draw(part_splits[0], (N, N, C), 1.0, 6.0, ((0, 4), (1, 4)))
    mask = set_ends((jax.random.randint(part_splits[1], (N,), 0, 8) < 7).astype(jnp.int32), jax.random.fold_in(part_splits[1], 1), 0, 1)
    in_weights = bell_draw(streams_of[2], (C, 4 * H), C ** -0.5, 0.5)
    gate_weight = bell_draw(streams_of[3], (C, C), C ** -0.5, 0.5)
    out_weight = bell_draw(streams_of[4], (H, C), H ** -0.5, 0.5)
    return {"pair": pair, "mask": mask, "in_weights": in_weights, "gate_weight": gate_weight, "out_weight": out_weight}


def normalize(values):
    values = values.astype(jnp.float32)
    mean = lax.optimization_barrier(jnp.mean(values, axis=-1, keepdims=True))
    centered = values - mean
    var = lax.optimization_barrier(jnp.mean(centered * centered, axis=-1, keepdims=True))
    return centered * jax.lax.rsqrt(var + 1e-05)

def reference(pair, mask, in_weights, gate_weight, out_weight):
    hidden = out_weight.shape[0]
    normed = normalize(pair).astype(jnp.bfloat16)
    flags = mask.astype(jnp.float32)
    both = flags[:, None, None] * flags[None, :, None]
    proj = jnp.einsum('abc,cd->abd', normed.astype(jnp.float32), in_weights.astype(jnp.float32))
    left = (jax.nn.sigmoid(proj[..., :hidden]) * proj[..., hidden:2 * hidden] * both).astype(jnp.bfloat16)
    right = (jax.nn.sigmoid(proj[..., 2 * hidden:3 * hidden]) * proj[..., 3 * hidden:] * both).astype(jnp.bfloat16)
    mixed = jnp.einsum('kic,kjc->ijc', left.astype(jnp.float32), right.astype(jnp.float32))
    mixed_normed = normalize(mixed).astype(jnp.bfloat16)
    gate = jax.nn.sigmoid(jnp.einsum('abc,cd->abd', normed.astype(jnp.float32), gate_weight.astype(jnp.float32)))
    value = jnp.einsum('abc,cd->abd', mixed_normed.astype(jnp.float32), out_weight.astype(jnp.float32))
    return (gate * value).astype(jnp.bfloat16)
```

```python
import jax
import jax.numpy as jnp
from jax import lax
from jax.sharding import PartitionSpec as P


def normalize(values):
    values = values.astype(jnp.float32)
    mean = jnp.mean(values, axis=-1, keepdims=True)
    centered = values - mean
    var = jnp.mean(centered * centered, axis=-1, keepdims=True)
    return centered * lax.rsqrt(var + 1e-05)


def project(block, weights):
    flat = block.reshape(-1, block.shape[-1])
    result = jnp.dot(flat, weights, preferred_element_type=jnp.float32)
    return result.reshape(block.shape[0], block.shape[1], weights.shape[1])


def gated(proj, first_flags, second_flags, hidden):
    both = first_flags[:, None, None] * second_flags[None, :, None]
    return (jax.nn.sigmoid(proj[..., :hidden]) * proj[..., hidden:] * both).astype(jnp.bfloat16)


def per_device(pair, mask, in_weights, gate_weight, out_weight):
    rows, cols, width = pair.shape
    hidden = out_weight.shape[0]
    row_at = lax.axis_index("row")
    col_at = lax.axis_index("col")
    flags = mask.astype(jnp.float32)
    row_flags = lax.dynamic_slice_in_dim(flags, row_at * rows, rows)
    col_flags = lax.dynamic_slice_in_dim(flags, col_at * cols, cols)
    normed = normalize(pair).astype(jnp.bfloat16)
    left_own = gated(project(normed, in_weights[:, : 2 * hidden]), row_flags, col_flags, hidden)
    left = lax.all_gather(left_own, "col", axis=0, tiled=False)
    right = gated(project(normed, in_weights[:, 2 * hidden :]), row_flags, col_flags, hidden)
    partial = jnp.einsum("nkic,kjc->nijc", left, right, preferred_element_type=jnp.float32)
    mixed = lax.psum_scatter(partial.astype(jnp.bfloat16), "row", scatter_dimension=0, tiled=False)
    mixed_normed = normalize(mixed).astype(jnp.bfloat16)
    gate = jax.nn.sigmoid(project(normed, gate_weight))
    value = project(mixed_normed, out_weight)
    return (gate * value).astype(jnp.bfloat16)


def solution(mesh):
    placed = (P(("parts", "row"), "col", None), P("parts"), P(), P(), P())
    return jax.shard_map(
        per_device,
        mesh=mesh,
        in_specs=placed,
        out_specs=P(("parts", "row"), "col", None),
        check_vma=False,
    )
```

```python
import functools

import jax
import jax.numpy as jnp
from jax import lax
from jax.experimental import pallas as pl
from jax.experimental.pallas import tpu as pltpu
from jax.sharding import PartitionSpec as P

MESH = pl.DeviceIdType.MESH
SLAB = 4
GROUP = 4


def normalize(values):
    values = values.astype(jnp.float32)
    mean = jnp.mean(values, axis=-1, keepdims=True)
    centered = values - mean
    var = jnp.mean(centered * centered, axis=-1, keepdims=True)
    return centered * lax.rsqrt(var + 1e-05)


def kernel(n_row, n_col, chunks, pair, row_flags, col_flags, in_w, gate_w, out_w, out,
           normed, left_all, right, left32, total, sums, arrived,
           own_sem, fwd_sem, left_sem, out_sem, in_sem):
    rows, cols, width = pair.shape
    hidden = out_w.shape[0]
    piece = rows // chunks
    chips = n_col // 2
    z = lax.axis_index("row")
    col = lax.axis_index("col")
    chip = col // 2
    core = col % 2
    sibling = 2 * chip + 1 - core

    barrier = pltpu.get_barrier_semaphore()
    pl.semaphore_signal(barrier, inc=1, device_id={"col": sibling}, device_id_type=MESH)
    for d in range(1, chips):
        pl.semaphore_signal(
            barrier, inc=1, device_id={"col": 2 * ((chip + d) % chips) + core}, device_id_type=MESH
        )

    @pl.when(z > 0)
    def _():
        pl.semaphore_signal(barrier, inc=1, device_id={"row": z - 1}, device_id_type=MESH)

    @pl.when(z < n_row - 1)
    def _():
        pl.semaphore_signal(barrier, inc=1, device_id={"row": z + 1}, device_id_type=MESH)

    def gated(proj, k0):
        value = jax.nn.sigmoid(proj[:, :hidden]) * proj[:, hidden:]
        value = value.reshape(SLAB, cols, hidden)
        flags = row_flags[pl.ds(k0, SLAB), :][:, None, :] * col_flags[...][None, :, :]
        return (value * flags).astype(jnp.bfloat16)

    @pl.loop(0, rows // SLAB)
    def _(s):
        k0 = s * SLAB
        own = normalize(pair[pl.ds(k0, SLAB)]).astype(jnp.bfloat16)
        normed[pl.ds(k0, SLAB)] = own
        proj = jnp.dot(own.reshape(SLAB * cols, width), in_w[:, : 2 * hidden], preferred_element_type=jnp.float32)
        left_all[col, pl.ds(k0, SLAB)] = gated(proj, k0)

    pl.semaphore_wait(barrier, chips + (z > 0).astype(jnp.int32) + (z < n_row - 1).astype(jnp.int32))

    def own_copy(d):
        target = sibling if d == 0 else 2 * ((chip + d) % chips) + core
        return pltpu.make_async_remote_copy(
            src_ref=left_all.at[col], dst_ref=left_all.at[col],
            send_sem=own_sem.at[d], recv_sem=left_sem.at[col],
            device_id={"col": target}, device_id_type=MESH,
        )

    def fwd_copy(d):
        source = 2 * ((chip - d + chips) % chips) + core
        return pltpu.make_async_remote_copy(
            src_ref=left_all.at[source], dst_ref=left_all.at[source],
            send_sem=fwd_sem.at[d], recv_sem=left_sem.at[source],
            device_id={"col": sibling}, device_id_type=MESH,
        )

    def wait_left(source):
        pltpu.make_async_remote_copy(
            src_ref=left_all.at[source], dst_ref=left_all.at[source],
            send_sem=own_sem.at[0], recv_sem=left_sem.at[source],
            device_id={"col": sibling}, device_id_type=MESH,
        ).wait_recv()

    for d in range(1, chips):
        own_copy(d).start()
    own_copy(0).start()

    @pl.loop(0, rows // SLAB)
    def _(s):
        k0 = s * SLAB
        own = normed[pl.ds(k0, SLAB)]
        proj = jnp.dot(own.reshape(SLAB * cols, width), in_w[:, 2 * hidden :], preferred_element_type=jnp.float32)
        right[pl.ds(k0, SLAB)] = gated(proj, k0).astype(jnp.float32)

    def product(place, i0):
        def add(k, accs):
            other = right[k]
            return tuple(accs[g] + left32[k, pl.ds(i0 + g, 1), :] * other for g in range(GROUP))

        zero = jnp.zeros((cols, hidden), jnp.float32)
        accs = lax.fori_loop(0, rows, add, (zero,) * GROUP, unroll=4)
        for g in range(GROUP):
            total[place, i0 + g] = accs[g]

    def sum_copy(r, c, up):
        span = pl.ds(c * piece, piece)
        if up:
            slot, target = r, z + 1
        else:
            slot, target = jnp.where(r == z - 1, n_row, r), z - 1
        return pltpu.make_async_remote_copy(
            src_ref=sums.at[r, span], dst_ref=arrived.at[slot, span],
            send_sem=out_sem.at[r, c], recv_sem=in_sem.at[slot, c],
            device_id={"row": target}, device_id_type=MESH,
        )

    def wait_sum(slot, c):
        span = pl.ds(c * piece, piece)
        pltpu.make_async_remote_copy(
            src_ref=sums.at[0, span], dst_ref=arrived.at[slot, span],
            send_sem=out_sem.at[0, c], recv_sem=in_sem.at[slot, c],
            device_id={"row": z}, device_id_type=MESH,
        ).wait_recv()

    def one_target(r):
        @pl.loop(0, rows // SLAB)
        def _(s):
            left32[pl.ds(s * SLAB, SLAB)] = left_all[r, pl.ds(s * SLAB, SLAB)].astype(jnp.float32)

        @pl.when(r == z)
        def _():
            @pl.loop(0, rows // GROUP)
            def _(s):
                product(1, s * GROUP)

        @pl.when(r != z)
        def _():
            inner = jnp.logical_or(jnp.logical_and(r > z, z > 0), jnp.logical_and(r < z, z < n_row - 1))

            @pl.loop(0, chunks)
            def _(c):
                @pl.loop(0, piece // GROUP)
                def _(s):
                    product(0, c * piece + s * GROUP)

                span = pl.ds(c * piece, piece)

                @pl.when(inner)
                def _():
                    wait_sum(r, c)
                    sums[r, span] = (total[0, span] + arrived[r, span].astype(jnp.float32)).astype(jnp.bfloat16)

                @pl.when(jnp.logical_not(inner))
                def _():
                    sums[r, span] = total[0, span].astype(jnp.bfloat16)

                @pl.when(r > z)
                def _():
                    sum_copy(r, c, True).start()

                @pl.when(r < z)
                def _():
                    sum_copy(r, c, False).start()

    for d in range(chips):
        other_chip = (chip - d + chips) % chips
        if d > 0:
            wait_left(2 * other_chip + core)
            fwd_copy(d).start()
        wait_left(2 * other_chip + 1 - core)
        low = (2 * other_chip < chips).astype(jnp.int32)

        @pl.loop(0, 2)
        def _(j):
            one_target(2 * other_chip + low * j + (1 - low) * (1 - j))

    @pl.loop(0, chunks)
    def _(c):
        span = pl.ds(c * piece, piece)

        @pl.when(z > 0)
        def _():
            wait_sum(z, c)
            total[1, span] += arrived[z, span].astype(jnp.float32)

        @pl.when(z < n_row - 1)
        def _():
            wait_sum(n_row, c)
            total[1, span] += arrived[n_row, span].astype(jnp.float32)

        @pl.loop(0, piece // SLAB)
        def _(s):
            at = pl.ds(c * piece + s * SLAB, SLAB)
            mixed = normalize(total[1, at]).astype(jnp.bfloat16).reshape(SLAB * cols, hidden)
            value = jnp.dot(mixed, out_w[...], preferred_element_type=jnp.float32)
            gate = jnp.dot(normed[at].reshape(SLAB * cols, width), gate_w[...], preferred_element_type=jnp.float32)
            out[at] = (jax.nn.sigmoid(gate) * value).astype(jnp.bfloat16).reshape(SLAB, cols, width)

    for d in range(chips):
        own_copy(d).wait_send()
        if d > 0:
            fwd_copy(d).wait_send()

    @pl.loop(0, n_row)
    def _(r):
        @pl.when(r != z)
        def _():
            @pl.loop(0, chunks)
            def _(c):
                sum_copy(r, c, True).wait_send()


def per_device(pair, mask, in_weights, gate_weight, out_weight):
    rows, cols, width = pair.shape
    hidden = out_weight.shape[0]
    n_row = lax.axis_size("row")
    n_col = lax.axis_size("col")
    chunks = 4
    flags = mask.astype(jnp.float32)
    row_flags = lax.dynamic_slice_in_dim(flags, lax.axis_index("row") * rows, rows)
    col_flags = lax.dynamic_slice_in_dim(flags, lax.axis_index("col") * cols, cols)
    row_flags = jnp.broadcast_to(row_flags[:, None], (rows, hidden))
    col_flags = jnp.broadcast_to(col_flags[:, None], (cols, hidden))
    vmem = pl.BlockSpec(memory_space=pltpu.VMEM)
    return pl.pallas_call(
        functools.partial(kernel, n_row, n_col, chunks),
        out_shape=jax.ShapeDtypeStruct(pair.shape, jnp.bfloat16),
        in_specs=[vmem] * 6,
        out_specs=vmem,
        scratch_shapes=[
            pltpu.VMEM((rows, cols, width), jnp.bfloat16),
            pltpu.VMEM((n_col, rows, cols, hidden), jnp.bfloat16),
            pltpu.VMEM((rows, cols, hidden), jnp.float32),
            pltpu.VMEM((rows, cols, hidden), jnp.float32),
            pltpu.VMEM((2, rows, cols, hidden), jnp.float32),
            pltpu.VMEM((n_row, rows, cols, hidden), jnp.bfloat16),
            pltpu.VMEM((n_row + 1, rows, cols, hidden), jnp.bfloat16),
            pltpu.SemaphoreType.DMA((n_col // 2,)),
            pltpu.SemaphoreType.DMA((n_col // 2,)),
            pltpu.SemaphoreType.DMA((n_col,)),
            pltpu.SemaphoreType.DMA((n_row, chunks)),
            pltpu.SemaphoreType.DMA((n_row + 1, chunks)),
        ],
        compiler_params=pltpu.CompilerParams(
            collective_id=0, has_side_effects=True, vmem_limit_bytes=48 * 1024 * 1024
        ),
    )(pair, row_flags, col_flags, in_weights, gate_weight, out_weight)


def solution(mesh):
    placed = (P(("parts", "row"), "col", None), P("parts"), P(), P(), P())
    return jax.shard_map(
        per_device,
        mesh=mesh,
        in_specs=placed,
        out_specs=P(("parts", "row"), "col", None),
        check_vma=False,
    )
```

```python
import functools

import jax
import jax.numpy as jnp
from jax import lax
from jax.experimental import pallas as pl
from jax.experimental.pallas import tpu as pltpu
from jax.sharding import PartitionSpec as P

MESH = pl.DeviceIdType.MESH
SLAB = 4
FIRST = 16
GROUP = 4


def normalize(values):
    values = values.astype(jnp.float32)
    mean = jnp.mean(values, axis=-1, keepdims=True)
    centered = values - mean
    var = jnp.mean(centered * centered, axis=-1, keepdims=True)
    return centered * lax.rsqrt(var + 1e-05)


def kernel(n_row, n_col, chunks, pair, row_flags, col_flags, in_w, gate_w, out_w, out,
           normed, left_all, right, left32, total, sums, arrived,
           own_sem, fwd_sem, left_sem, out_sem, in_sem):
    rows, cols, width = pair.shape
    hidden = out_w.shape[0]
    piece = rows // chunks
    chips = n_col // 2
    z = lax.axis_index("row")
    col = lax.axis_index("col")
    chip = col // 2
    core = col % 2
    sibling = 2 * chip + 1 - core

    barrier = pltpu.get_barrier_semaphore()
    pl.semaphore_signal(barrier, inc=1, device_id={"col": sibling}, device_id_type=MESH)
    for d in range(1, chips):
        pl.semaphore_signal(
            barrier, inc=1, device_id={"col": 2 * ((chip + d) % chips) + core}, device_id_type=MESH
        )

    @pl.when(z > 0)
    def _():
        pl.semaphore_signal(barrier, inc=1, device_id={"row": z - 1}, device_id_type=MESH)

    @pl.when(z < n_row - 1)
    def _():
        pl.semaphore_signal(barrier, inc=1, device_id={"row": z + 1}, device_id_type=MESH)

    def gated(proj, k0):
        value = jax.nn.sigmoid(proj[:, :hidden]) * proj[:, hidden:]
        value = value.reshape(FIRST, cols, hidden)
        flags = row_flags[pl.ds(k0, FIRST), :][:, None, :] * col_flags[...][None, :, :]
        return (value * flags).astype(jnp.bfloat16)

    @pl.loop(0, rows // FIRST)
    def _(s):
        k0 = s * FIRST
        own = normalize(pair[pl.ds(k0, FIRST)]).astype(jnp.bfloat16)
        normed[pl.ds(k0, FIRST)] = own
        proj = jnp.dot(own.reshape(FIRST * cols, width), in_w[:, : 2 * hidden], preferred_element_type=jnp.float32)
        left_all[col, pl.ds(k0, FIRST)] = gated(proj, k0)

    pl.semaphore_wait(barrier, chips + (z > 0).astype(jnp.int32) + (z < n_row - 1).astype(jnp.int32))

    def own_copy(d):
        target = sibling if d == 0 else 2 * ((chip + d) % chips) + core
        return pltpu.make_async_remote_copy(
            src_ref=left_all.at[col], dst_ref=left_all.at[col],
            send_sem=own_sem.at[d], recv_sem=left_sem.at[col],
            device_id={"col": target}, device_id_type=MESH,
        )

    def fwd_copy(d):
        source = 2 * ((chip - d + chips) % chips) + core
        return pltpu.make_async_remote_copy(
            src_ref=left_all.at[source], dst_ref=left_all.at[source],
            send_sem=fwd_sem.at[d], recv_sem=left_sem.at[source],
            device_id={"col": sibling}, device_id_type=MESH,
        )

    def wait_left(source):
        pltpu.make_async_remote_copy(
            src_ref=left_all.at[source], dst_ref=left_all.at[source],
            send_sem=own_sem.at[0], recv_sem=left_sem.at[source],
            device_id={"col": sibling}, device_id_type=MESH,
        ).wait_recv()

    for d in range(1, chips):
        own_copy(d).start()
    own_copy(0).start()

    @pl.loop(0, rows // FIRST)
    def _(s):
        k0 = s * FIRST
        own = normed[pl.ds(k0, FIRST)]
        proj = jnp.dot(own.reshape(FIRST * cols, width), in_w[:, 2 * hidden :], preferred_element_type=jnp.float32)
        right[pl.ds(k0, FIRST)] = gated(proj, k0).astype(jnp.float32)

    def product(i0):
        def add(k, accs):
            other = right[k]
            return tuple(accs[g] + left32[k, pl.ds(i0 + g, 1), :] * other for g in range(GROUP))

        zero = jnp.zeros((cols, hidden), jnp.float32)
        return lax.fori_loop(0, rows, add, (zero,) * GROUP, unroll=8)

    def sum_copy(r, c, up):
        span = pl.ds(c * piece, piece)
        if up:
            slot, target = r, z + 1
        else:
            slot, target = jnp.where(r == z - 1, n_row, r), z - 1
        return pltpu.make_async_remote_copy(
            src_ref=sums.at[r, span], dst_ref=arrived.at[slot, span],
            send_sem=out_sem.at[r, c], recv_sem=in_sem.at[slot, c],
            device_id={"row": target}, device_id_type=MESH,
        )

    def wait_sum(slot, c):
        span = pl.ds(c * piece, piece)
        pltpu.make_async_remote_copy(
            src_ref=sums.at[0, span], dst_ref=arrived.at[slot, span],
            send_sem=out_sem.at[0, c], recv_sem=in_sem.at[slot, c],
            device_id={"row": z}, device_id_type=MESH,
        ).wait_recv()

    def finish(c):
        span = pl.ds(c * piece, piece)

        @pl.when(z > 0)
        def _():
            wait_sum(z, c)
            total[span] += arrived[z, span].astype(jnp.float32)

        @pl.when(z < n_row - 1)
        def _():
            wait_sum(n_row, c)
            total[span] += arrived[n_row, span].astype(jnp.float32)

        @pl.loop(0, piece // SLAB)
        def _(s):
            at = pl.ds(c * piece + s * SLAB, SLAB)
            mixed = normalize(total[at]).astype(jnp.bfloat16).reshape(SLAB * cols, hidden)
            value = jnp.dot(mixed, out_w[...], preferred_element_type=jnp.float32)
            gate = jnp.dot(normed[at].reshape(SLAB * cols, width), gate_w[...], preferred_element_type=jnp.float32)
            out[at] = (jax.nn.sigmoid(gate) * value).astype(jnp.bfloat16).reshape(SLAB, cols, width)

    def one_target(r, closing):
        @pl.loop(0, rows // FIRST)
        def _(s):
            left32[pl.ds(s * FIRST, FIRST)] = left_all[r, pl.ds(s * FIRST, FIRST)].astype(jnp.float32)

        @pl.when(r == z)
        def _():
            @pl.loop(0, rows // GROUP)
            def _(s):
                accs = product(s * GROUP)
                for g in range(GROUP):
                    total[s * GROUP + g] = accs[g]

        @pl.when(r != z)
        def _():
            inner = jnp.logical_or(jnp.logical_and(r > z, z > 0), jnp.logical_and(r < z, z < n_row - 1))

            @pl.loop(0, chunks)
            def _(c):
                @pl.when(closing)
                def _():
                    finish(c)

                accs = product(c * piece)

                @pl.when(inner)
                def _():
                    wait_sum(r, c)
                    for g in range(GROUP):
                        at = c * piece + g
                        sums[r, at] = (accs[g] + arrived[r, at].astype(jnp.float32)).astype(jnp.bfloat16)

                @pl.when(jnp.logical_not(inner))
                def _():
                    for g in range(GROUP):
                        sums[r, c * piece + g] = accs[g].astype(jnp.bfloat16)

                @pl.when(r > z)
                def _():
                    sum_copy(r, c, True).start()

                @pl.when(r < z)
                def _():
                    sum_copy(r, c, False).start()

    for d in range(chips):
        other_chip = (chip - d + chips) % chips
        if d > 0:
            wait_left(2 * other_chip + core)
            fwd_copy(d).start()
        wait_left(2 * other_chip + 1 - core)
        low = (2 * other_chip < chips).astype(jnp.int32)
        first = 2 * other_chip + 1 - low
        last = 2 * other_chip + low
        swap = (first == z).astype(jnp.int32)

        @pl.loop(0, 2)
        def _(j):
            at = (j + swap) % 2
            target = at * last + (1 - at) * first
            one_target(target, jnp.logical_and(jnp.logical_and(j == 1, d == chips - 1), jnp.logical_and(first != z, last != z)))

    early = jnp.logical_and(last != z, first != z)

    @pl.when(jnp.logical_not(early))
    def _():
        pl.loop(0, chunks)(finish)

    for d in range(chips):
        own_copy(d).wait_send()
        if d > 0:
            fwd_copy(d).wait_send()

    @pl.loop(0, n_row)
    def _(r):
        @pl.when(r != z)
        def _():
            @pl.loop(0, chunks)
            def _(c):
                sum_copy(r, c, True).wait_send()


def per_device(pair, mask, in_weights, gate_weight, out_weight):
    rows, cols, width = pair.shape
    hidden = out_weight.shape[0]
    n_row = lax.axis_size("row")
    n_col = lax.axis_size("col")
    chunks = rows // GROUP
    flags = mask.astype(jnp.float32)
    row_flags = lax.dynamic_slice_in_dim(flags, lax.axis_index("row") * rows, rows)
    col_flags = lax.dynamic_slice_in_dim(flags, lax.axis_index("col") * cols, cols)
    row_flags = jnp.broadcast_to(row_flags[:, None], (rows, hidden))
    col_flags = jnp.broadcast_to(col_flags[:, None], (cols, hidden))
    vmem = pl.BlockSpec(memory_space=pltpu.VMEM)
    return pl.pallas_call(
        functools.partial(kernel, n_row, n_col, chunks),
        out_shape=jax.ShapeDtypeStruct(pair.shape, jnp.bfloat16),
        in_specs=[vmem] * 6,
        out_specs=vmem,
        scratch_shapes=[
            pltpu.VMEM((rows, cols, width), jnp.bfloat16),
            pltpu.VMEM((n_col, rows, cols, hidden), jnp.bfloat16),
            pltpu.VMEM((rows, cols, hidden), jnp.float32),
            pltpu.VMEM((rows, cols, hidden), jnp.float32),
            pltpu.VMEM((rows, cols, hidden), jnp.float32),
            pltpu.VMEM((n_row, rows, cols, hidden), jnp.bfloat16),
            pltpu.VMEM((n_row + 1, rows, cols, hidden), jnp.bfloat16),
            pltpu.SemaphoreType.DMA((n_col // 2,)),
            pltpu.SemaphoreType.DMA((n_col // 2,)),
            pltpu.SemaphoreType.DMA((n_col,)),
            pltpu.SemaphoreType.DMA((n_row, chunks)),
            pltpu.SemaphoreType.DMA((n_row + 1, chunks)),
        ],
        compiler_params=pltpu.CompilerParams(
            collective_id=0, has_side_effects=True, vmem_limit_bytes=48 * 1024 * 1024
        ),
    )(pair, row_flags, col_flags, in_weights, gate_weight, out_weight)


def solution(mesh):
    placed = (P(("parts", "row"), "col", None), P("parts"), P(), P(), P())
    return jax.shard_map(
        per_device,
        mesh=mesh,
        in_specs=placed,
        out_specs=P(("parts", "row"), "col", None),
        check_vma=False,
    )
```

```python
import functools

import jax
import jax.numpy as jnp
from jax import lax
from jax.experimental import pallas as pl
from jax.experimental.pallas import tpu as pltpu
from jax.sharding import PartitionSpec as P

MESH = pl.DeviceIdType.MESH
SLAB = 4
FIRST = 16
GROUP = 4


def normalize(values):
    values = values.astype(jnp.float32)
    mean = jnp.mean(values, axis=-1, keepdims=True)
    centered = values - mean
    var = jnp.mean(centered * centered, axis=-1, keepdims=True)
    return centered * lax.rsqrt(var + 1e-05)


def kernel(n_row, n_col, chunks, pair, row_flags, col_flags, in_w, gate_w, out_w, out,
           normed, left_all, right, left32, total, sums, arrived,
           own_sem, fwd_sem, left_sem, out_sem, in_sem):
    rows, cols, width = pair.shape
    hidden = out_w.shape[0]
    piece = rows // chunks
    chips = n_col // 2
    z = lax.axis_index("row")
    col = lax.axis_index("col")
    chip = col // 2
    core = col % 2
    sibling = 2 * chip + 1 - core

    barrier = pltpu.get_barrier_semaphore()
    pl.semaphore_signal(barrier, inc=1, device_id={"col": sibling}, device_id_type=MESH)
    for d in range(1, chips):
        pl.semaphore_signal(
            barrier, inc=1, device_id={"col": 2 * ((chip + d) % chips) + core}, device_id_type=MESH
        )

    @pl.when(z > 0)
    def _():
        pl.semaphore_signal(barrier, inc=1, device_id={"row": z - 1}, device_id_type=MESH)

    @pl.when(z < n_row - 1)
    def _():
        pl.semaphore_signal(barrier, inc=1, device_id={"row": z + 1}, device_id_type=MESH)

    def gated(proj, k0):
        value = jax.nn.sigmoid(proj[:, :hidden]) * proj[:, hidden:]
        value = value.reshape(FIRST, cols, hidden)
        flags = row_flags[pl.ds(k0, FIRST), :][:, None, :] * col_flags[...][None, :, :]
        return (value * flags).astype(jnp.bfloat16)

    @pl.loop(0, rows // FIRST)
    def _(s):
        k0 = s * FIRST
        own = normalize(pair[pl.ds(k0, FIRST)]).astype(jnp.bfloat16)
        normed[pl.ds(k0, FIRST)] = own
        proj = jnp.dot(own.reshape(FIRST * cols, width), in_w[:, : 2 * hidden], preferred_element_type=jnp.float32)
        left_all[col, pl.ds(k0, FIRST)] = gated(proj, k0)

    pl.semaphore_wait(barrier, chips + (z > 0).astype(jnp.int32) + (z < n_row - 1).astype(jnp.int32))

    def own_copy(d):
        target = sibling if d == 0 else 2 * ((chip + d) % chips) + core
        return pltpu.make_async_remote_copy(
            src_ref=left_all.at[col], dst_ref=left_all.at[col],
            send_sem=own_sem.at[d], recv_sem=left_sem.at[col],
            device_id={"col": target}, device_id_type=MESH,
        )

    def fwd_copy(d):
        source = 2 * ((chip - d + chips) % chips) + core
        return pltpu.make_async_remote_copy(
            src_ref=left_all.at[source], dst_ref=left_all.at[source],
            send_sem=fwd_sem.at[d], recv_sem=left_sem.at[source],
            device_id={"col": sibling}, device_id_type=MESH,
        )

    def wait_left(source):
        pltpu.make_async_remote_copy(
            src_ref=left_all.at[source], dst_ref=left_all.at[source],
            send_sem=own_sem.at[0], recv_sem=left_sem.at[source],
            device_id={"col": sibling}, device_id_type=MESH,
        ).wait_recv()

    for d in range(1, chips):
        own_copy(d).start()
    own_copy(0).start()

    @pl.loop(0, rows // FIRST)
    def _(s):
        k0 = s * FIRST
        own = normed[pl.ds(k0, FIRST)]
        proj = jnp.dot(own.reshape(FIRST * cols, width), in_w[:, 2 * hidden :], preferred_element_type=jnp.float32)
        right[pl.ds(k0, FIRST)] = gated(proj, k0).astype(jnp.float32)

    def product(i0):
        def add(k, accs):
            other = right[k]
            return tuple(accs[g] + left32[k, pl.ds(i0 + g, 1), :] * other for g in range(GROUP))

        zero = jnp.zeros((cols, hidden), jnp.float32)
        return lax.fori_loop(0, rows, add, (zero,) * GROUP, unroll=16)

    def sum_copy(r, c, up):
        span = pl.ds(c * piece, piece)
        if up:
            slot, target = r, z + 1
        else:
            slot, target = jnp.where(r == z - 1, n_row, r), z - 1
        return pltpu.make_async_remote_copy(
            src_ref=sums.at[r, span], dst_ref=arrived.at[slot, span],
            send_sem=out_sem.at[r, c], recv_sem=in_sem.at[slot, c],
            device_id={"row": target}, device_id_type=MESH,
        )

    def wait_sum(slot, c):
        span = pl.ds(c * piece, piece)
        pltpu.make_async_remote_copy(
            src_ref=sums.at[0, span], dst_ref=arrived.at[slot, span],
            send_sem=out_sem.at[0, c], recv_sem=in_sem.at[slot, c],
            device_id={"row": z}, device_id_type=MESH,
        ).wait_recv()

    def finish(c):
        span = pl.ds(c * piece, piece)

        @pl.when(z > 0)
        def _():
            wait_sum(z, c)
            total[span] += arrived[z, span].astype(jnp.float32)

        @pl.when(z < n_row - 1)
        def _():
            wait_sum(n_row, c)
            total[span] += arrived[n_row, span].astype(jnp.float32)

        @pl.loop(0, piece // SLAB)
        def _(s):
            at = pl.ds(c * piece + s * SLAB, SLAB)
            mixed = normalize(total[at]).astype(jnp.bfloat16).reshape(SLAB * cols, hidden)
            value = jnp.dot(mixed, out_w[...], preferred_element_type=jnp.float32)
            gate = jnp.dot(normed[at].reshape(SLAB * cols, width), gate_w[...], preferred_element_type=jnp.float32)
            out[at] = (jax.nn.sigmoid(gate) * value).astype(jnp.bfloat16).reshape(SLAB, cols, width)

    def one_target(r, closing):
        @pl.loop(0, rows // FIRST)
        def _(s):
            left32[pl.ds(s * FIRST, FIRST)] = left_all[r, pl.ds(s * FIRST, FIRST)].astype(jnp.float32)

        @pl.when(r == z)
        def _():
            @pl.loop(0, rows // GROUP)
            def _(s):
                accs = product(s * GROUP)
                for g in range(GROUP):
                    total[s * GROUP + g] = accs[g]

        @pl.when(r != z)
        def _():
            inner = jnp.logical_or(jnp.logical_and(r > z, z > 0), jnp.logical_and(r < z, z < n_row - 1))

            @pl.loop(0, chunks)
            def _(c):
                @pl.when(closing)
                def _():
                    finish(c)

                accs = product(c * piece)

                @pl.when(inner)
                def _():
                    wait_sum(r, c)
                    for g in range(GROUP):
                        at = c * piece + g
                        sums[r, at] = (accs[g] + arrived[r, at].astype(jnp.float32)).astype(jnp.bfloat16)

                @pl.when(jnp.logical_not(inner))
                def _():
                    for g in range(GROUP):
                        sums[r, c * piece + g] = accs[g].astype(jnp.bfloat16)

                @pl.when(r > z)
                def _():
                    sum_copy(r, c, True).start()

                @pl.when(r < z)
                def _():
                    sum_copy(r, c, False).start()

    for d in range(chips):
        other_chip = (chip - d + chips) % chips
        if d > 0:
            wait_left(2 * other_chip + core)
            fwd_copy(d).start()
        wait_left(2 * other_chip + 1 - core)
        low = (2 * other_chip < chips).astype(jnp.int32)
        first = 2 * other_chip + 1 - low
        last = 2 * other_chip + low
        swap = (first == z).astype(jnp.int32)

        @pl.loop(0, 2)
        def _(j):
            at = (j + swap) % 2
            target = at * last + (1 - at) * first
            one_target(target, jnp.logical_and(jnp.logical_and(j == 1, d == chips - 1), jnp.logical_and(first != z, last != z)))

    early = jnp.logical_and(last != z, first != z)

    @pl.when(jnp.logical_not(early))
    def _():
        pl.loop(0, chunks)(finish)

    for d in range(chips):
        own_copy(d).wait_send()
        if d > 0:
            fwd_copy(d).wait_send()

    @pl.loop(0, n_row)
    def _(r):
        @pl.when(r != z)
        def _():
            @pl.loop(0, chunks)
            def _(c):
                span = pl.ds(c * piece, piece)
                pltpu.make_async_remote_copy(
                    src_ref=sums.at[r, span], dst_ref=arrived.at[r, span],
                    send_sem=out_sem.at[r, c], recv_sem=in_sem.at[r, c],
                    device_id={"row": z}, device_id_type=MESH,
                ).wait_send()


def per_device(pair, mask, in_weights, gate_weight, out_weight):
    rows, cols, width = pair.shape
    hidden = out_weight.shape[0]
    n_row = lax.axis_size("row")
    n_col = lax.axis_size("col")
    chunks = rows // GROUP
    flags = mask.astype(jnp.float32)
    row_flags = lax.dynamic_slice_in_dim(flags, lax.axis_index("row") * rows, rows)
    col_flags = lax.dynamic_slice_in_dim(flags, lax.axis_index("col") * cols, cols)
    row_flags = jnp.broadcast_to(row_flags[:, None], (rows, hidden))
    col_flags = jnp.broadcast_to(col_flags[:, None], (cols, hidden))
    vmem = pl.BlockSpec(memory_space=pltpu.VMEM)
    return pl.pallas_call(
        functools.partial(kernel, n_row, n_col, chunks),
        out_shape=jax.ShapeDtypeStruct(pair.shape, jnp.bfloat16),
        in_specs=[vmem] * 6,
        out_specs=vmem,
        scratch_shapes=[
            pltpu.VMEM((rows, cols, width), jnp.bfloat16),
            pltpu.VMEM((n_col, rows, cols, hidden), jnp.bfloat16),
            pltpu.VMEM((rows, cols, hidden), jnp.float32),
            pltpu.VMEM((rows, cols, hidden), jnp.float32),
            pltpu.VMEM((rows, cols, hidden), jnp.float32),
            pltpu.VMEM((n_row, rows, cols, hidden), jnp.bfloat16),
            pltpu.VMEM((n_row + 1, rows, cols, hidden), jnp.bfloat16),
            pltpu.SemaphoreType.DMA((n_col // 2,)),
            pltpu.SemaphoreType.DMA((n_col // 2,)),
            pltpu.SemaphoreType.DMA((n_col,)),
            pltpu.SemaphoreType.DMA((n_row, chunks)),
            pltpu.SemaphoreType.DMA((n_row + 1, chunks)),
        ],
        compiler_params=pltpu.CompilerParams(
            collective_id=0, has_side_effects=True, vmem_limit_bytes=48 * 1024 * 1024
        ),
    )(pair, row_flags, col_flags, in_weights, gate_weight, out_weight)


def solution(mesh):
    placed = (P(("parts", "row"), "col", None), P("parts"), P(), P(), P())
    return jax.shard_map(
        per_device,
        mesh=mesh,
        in_specs=placed,
        out_specs=P(("parts", "row"), "col", None),
        check_vma=False,
    )
```

```python
import functools

import jax
import jax.numpy as jnp
from jax import lax
from jax.experimental import pallas as pl
from jax.experimental.pallas import tpu as pltpu
from jax.sharding import PartitionSpec as P

MESH = pl.DeviceIdType.MESH
SLAB = 4
FIRST = 16
GROUP = 4


def normalize(values):
    values = values.astype(jnp.float32)
    mean = jnp.mean(values, axis=-1, keepdims=True)
    centered = values - mean
    var = jnp.mean(centered * centered, axis=-1, keepdims=True)
    return centered * lax.rsqrt(var + 1e-05)


def kernel(n_row, n_col, chunks, pair, row_flags, col_flags, in_w, gate_w, out_w, out,
           gates, normed, left_all, right, left32, total, sums, arrived,
           own_sem, fwd_sem, left_sem, out_sem, in_sem):
    rows, cols, width = pair.shape
    hidden = out_w.shape[0]
    piece = rows // chunks
    chips = n_col // 2
    z = lax.axis_index("row")
    col = lax.axis_index("col")
    chip = col // 2
    core = col % 2
    sibling = 2 * chip + 1 - core

    barrier = pltpu.get_barrier_semaphore()
    pl.semaphore_signal(barrier, inc=1, device_id={"col": sibling}, device_id_type=MESH)
    for d in range(1, chips):
        pl.semaphore_signal(
            barrier, inc=1, device_id={"col": 2 * ((chip + d) % chips) + core}, device_id_type=MESH
        )

    @pl.when(z > 0)
    def _():
        pl.semaphore_signal(barrier, inc=1, device_id={"row": z - 1}, device_id_type=MESH)

    @pl.when(z < n_row - 1)
    def _():
        pl.semaphore_signal(barrier, inc=1, device_id={"row": z + 1}, device_id_type=MESH)

    def gated(proj, k0):
        value = jax.nn.sigmoid(proj[:, :hidden]) * proj[:, hidden:]
        value = value.reshape(FIRST, cols, hidden)
        flags = row_flags[pl.ds(k0, FIRST), :][:, None, :] * col_flags[...][None, :, :]
        return (value * flags).astype(jnp.bfloat16)

    @pl.loop(0, rows // FIRST)
    def _(s):
        k0 = s * FIRST
        own = normalize(pair[pl.ds(k0, FIRST)]).astype(jnp.bfloat16)
        normed[pl.ds(k0, FIRST)] = own
        proj = jnp.dot(own.reshape(FIRST * cols, width), in_w[:, : 2 * hidden], preferred_element_type=jnp.float32)
        left_all[col, pl.ds(k0, FIRST)] = gated(proj, k0)

    pl.semaphore_wait(barrier, chips + (z > 0).astype(jnp.int32) + (z < n_row - 1).astype(jnp.int32))

    def own_copy(d):
        target = sibling if d == 0 else 2 * ((chip + d) % chips) + core
        return pltpu.make_async_remote_copy(
            src_ref=left_all.at[col], dst_ref=left_all.at[col],
            send_sem=own_sem.at[d], recv_sem=left_sem.at[col],
            device_id={"col": target}, device_id_type=MESH,
        )

    def fwd_copy(d):
        source = 2 * ((chip - d + chips) % chips) + core
        return pltpu.make_async_remote_copy(
            src_ref=left_all.at[source], dst_ref=left_all.at[source],
            send_sem=fwd_sem.at[d], recv_sem=left_sem.at[source],
            device_id={"col": sibling}, device_id_type=MESH,
        )

    def wait_left(source):
        pltpu.make_async_remote_copy(
            src_ref=left_all.at[source], dst_ref=left_all.at[source],
            send_sem=own_sem.at[0], recv_sem=left_sem.at[source],
            device_id={"col": sibling}, device_id_type=MESH,
        ).wait_recv()

    for d in range(1, chips):
        own_copy(d).start()
    own_copy(0).start()

    @pl.loop(0, rows // FIRST)
    def _(s):
        k0 = s * FIRST
        own = normed[pl.ds(k0, FIRST)]
        proj = jnp.dot(own.reshape(FIRST * cols, width), in_w[:, 2 * hidden :], preferred_element_type=jnp.float32)
        right[pl.ds(k0, FIRST)] = gated(proj, k0).astype(jnp.float32)

    def product(i0):
        def add(k, accs):
            other = right[k]
            return tuple(accs[g] + left32[k, pl.ds(i0 + g, 1), :] * other for g in range(GROUP))

        zero = jnp.zeros((cols, hidden), jnp.float32)
        return lax.fori_loop(0, rows, add, (zero,) * GROUP, unroll=16)

    def sum_copy(r, c, up):
        span = pl.ds(c * piece, piece)
        if up:
            slot, target = r, z + 1
        else:
            slot, target = jnp.where(r == z - 1, n_row, r), z - 1
        return pltpu.make_async_remote_copy(
            src_ref=sums.at[r, span], dst_ref=arrived.at[slot, span],
            send_sem=out_sem.at[r, c], recv_sem=in_sem.at[slot, c],
            device_id={"row": target}, device_id_type=MESH,
        )

    def wait_sum(slot, c):
        span = pl.ds(c * piece, piece)
        pltpu.make_async_remote_copy(
            src_ref=sums.at[0, span], dst_ref=arrived.at[slot, span],
            send_sem=out_sem.at[0, c], recv_sem=in_sem.at[slot, c],
            device_id={"row": z}, device_id_type=MESH,
        ).wait_recv()

    def finish(c):
        span = pl.ds(c * piece, piece)

        @pl.when(z > 0)
        def _():
            wait_sum(z, c)
            total[span] += arrived[z, span].astype(jnp.float32)

        @pl.when(z < n_row - 1)
        def _():
            wait_sum(n_row, c)
            total[span] += arrived[n_row, span].astype(jnp.float32)

        @pl.loop(0, piece // SLAB)
        def _(s):
            at = pl.ds(c * piece + s * SLAB, SLAB)
            mixed = normalize(total[at]).astype(jnp.bfloat16).reshape(SLAB * cols, hidden)
            value = jnp.dot(mixed, out_w[...], preferred_element_type=jnp.float32)
            gate = gates[at].reshape(SLAB * cols, width)
            out[at] = (gate * value).astype(jnp.bfloat16).reshape(SLAB, cols, width)

    def one_target(r, closing):
        @pl.loop(0, rows // FIRST)
        def _(s):
            left32[pl.ds(s * FIRST, FIRST)] = left_all[r, pl.ds(s * FIRST, FIRST)].astype(jnp.float32)

        @pl.when(r == z)
        def _():
            @pl.loop(0, rows // GROUP)
            def _(s):
                accs = product(s * GROUP)
                for g in range(GROUP):
                    total[s * GROUP + g] = accs[g]

        @pl.when(r != z)
        def _():
            inner = jnp.logical_or(jnp.logical_and(r > z, z > 0), jnp.logical_and(r < z, z < n_row - 1))

            @pl.loop(0, chunks)
            def _(c):
                @pl.when(closing)
                def _():
                    finish(c)

                accs = product(c * piece)

                @pl.when(inner)
                def _():
                    wait_sum(r, c)
                    for g in range(GROUP):
                        at = c * piece + g
                        sums[r, at] = (accs[g] + arrived[r, at].astype(jnp.float32)).astype(jnp.bfloat16)

                @pl.when(jnp.logical_not(inner))
                def _():
                    for g in range(GROUP):
                        sums[r, c * piece + g] = accs[g].astype(jnp.bfloat16)

                @pl.when(r > z)
                def _():
                    sum_copy(r, c, True).start()

                @pl.when(r < z)
                def _():
                    sum_copy(r, c, False).start()

    for d in range(chips):
        other_chip = (chip - d + chips) % chips
        if d == chips - 1:

            @pl.loop(0, rows // FIRST)
            def _(s):
                at = pl.ds(s * FIRST, FIRST)
                flat = normed[at].reshape(FIRST * cols, width)
                gate = jnp.dot(flat, gate_w[...], preferred_element_type=jnp.float32)
                gates[at] = jax.nn.sigmoid(gate).reshape(FIRST, cols, width)

        if d > 0:
            wait_left(2 * other_chip + core)
            fwd_copy(d).start()
        wait_left(2 * other_chip + 1 - core)
        low = (2 * other_chip < chips).astype(jnp.int32)
        first = 2 * other_chip + 1 - low
        last = 2 * other_chip + low
        swap = (first == z).astype(jnp.int32)

        @pl.loop(0, 2)
        def _(j):
            at = (j + swap) % 2
            target = at * last + (1 - at) * first
            one_target(target, jnp.logical_and(jnp.logical_and(j == 1, d == chips - 1), jnp.logical_and(first != z, last != z)))

    early = jnp.logical_and(last != z, first != z)

    @pl.when(jnp.logical_not(early))
    def _():
        pl.loop(0, chunks)(finish)

    for d in range(chips):
        own_copy(d).wait_send()
        if d > 0:
            fwd_copy(d).wait_send()

    @pl.loop(0, n_row)
    def _(r):
        @pl.when(r != z)
        def _():
            @pl.loop(0, chunks)
            def _(c):
                span = pl.ds(c * piece, piece)
                pltpu.make_async_remote_copy(
                    src_ref=sums.at[r, span], dst_ref=arrived.at[r, span],
                    send_sem=out_sem.at[r, c], recv_sem=in_sem.at[r, c],
                    device_id={"row": z}, device_id_type=MESH,
                ).wait_send()


def per_device(pair, mask, in_weights, gate_weight, out_weight):
    rows, cols, width = pair.shape
    hidden = out_weight.shape[0]
    n_row = lax.axis_size("row")
    n_col = lax.axis_size("col")
    chunks = rows // GROUP
    flags = mask.astype(jnp.float32)
    row_flags = lax.dynamic_slice_in_dim(flags, lax.axis_index("row") * rows, rows)
    col_flags = lax.dynamic_slice_in_dim(flags, lax.axis_index("col") * cols, cols)
    row_flags = jnp.broadcast_to(row_flags[:, None], (rows, hidden))
    col_flags = jnp.broadcast_to(col_flags[:, None], (cols, hidden))
    vmem = pl.BlockSpec(memory_space=pltpu.VMEM)
    return pl.pallas_call(
        functools.partial(kernel, n_row, n_col, chunks),
        out_shape=jax.ShapeDtypeStruct(pair.shape, jnp.bfloat16),
        in_specs=[vmem] * 6,
        out_specs=vmem,
        scratch_shapes=[
            pltpu.VMEM((rows, cols, width), jnp.float32),
            pltpu.VMEM((rows, cols, width), jnp.bfloat16),
            pltpu.VMEM((n_col, rows, cols, hidden), jnp.bfloat16),
            pltpu.VMEM((rows, cols, hidden), jnp.float32),
            pltpu.VMEM((rows, cols, hidden), jnp.float32),
            pltpu.VMEM((rows, cols, hidden), jnp.float32),
            pltpu.VMEM((n_row, rows, cols, hidden), jnp.bfloat16),
            pltpu.VMEM((n_row + 1, rows, cols, hidden), jnp.bfloat16),
            pltpu.SemaphoreType.DMA((n_col // 2,)),
            pltpu.SemaphoreType.DMA((n_col // 2,)),
            pltpu.SemaphoreType.DMA((n_col,)),
            pltpu.SemaphoreType.DMA((n_row, chunks)),
            pltpu.SemaphoreType.DMA((n_row + 1, chunks)),
        ],
        compiler_params=pltpu.CompilerParams(
            collective_id=0, has_side_effects=True, vmem_limit_bytes=48 * 1024 * 1024
        ),
    )(pair, row_flags, col_flags, in_weights, gate_weight, out_weight)


def solution(mesh):
    placed = (P(("parts", "row"), "col", None), P("parts"), P(), P(), P())
    return jax.shard_map(
        per_device,
        mesh=mesh,
        in_specs=placed,
        out_specs=P(("parts", "row"), "col", None),
        check_vma=False,
    )
```
